512 devices in a mesh: row: 16 (over x_hi, z), col: 16 (over y, core), rep: 2 (over x_lo).
Axes of the slice: x: 4 (x_hi: 2, x_lo: 2; x = x_hi * 2 + x_lo), y: 8, z: 8, core: 2. Of those that a mesh axis runs over, the one named last changes fastest.
Arguments:
- grad_parts: bfloat16 [2, 4608, 4608], P('rep', 'row', 'col'), may hold values from -6 to 6
- basis_left: bfloat16 [4608, 4608], P(('col', 'rep'), 'row'), may hold values from -0.09375 to 0.09375
- basis_right: bfloat16 [4608, 4608], P(('row', 'rep'), 'col'), may hold values from -0.09375 to 0.09375
- first_moment: float32 [4608, 4608], P(('row', 'rep'), 'col'), may hold values from -6 to 6
- second_moment: float32 [4608, 4608], P(('row', 'rep'), 'col'), may hold values from 0.5 to 4
Outputs:
- update: float32 [4608, 4608], P(('row', 'rep'), 'col')
- new_first: float32 [4608, 4608], P(('row', 'rep'), 'col')
- new_second: float32 [4608, 4608], P(('row', 'rep'), 'col')
The draws below stay inside these ranges and needn't reach their ends.
All inputs are finite; a program needn't handle non-finite values.
Results may differ from the reference program's by a relative error of at most 0.0041.
Values may be sent and summed in bfloat16 or wider, within the bound.
No kernel may reach another device: no remote copies, remote signals or barrier semaphores. Data moves between devices by JAX's collectives and lax.ppermute only.
A program may use at most 64 MiB of HBM per device.

```python
import math
import jax
import jax.numpy as jnp
from jax import lax

D = 4608
N_REP = 2


def shard_levels(key, shape, pieces, low, largest):
    level, own = 1.0, jax.random.fold_in(key, 6)
    for dim, blocks in pieces:
        draws = jnp.exp(jax.random.uniform(jax.random.fold_in(own, dim), (blocks,), jnp.float32, low / len(pieces), largest / len(pieces)))
        level = level * jnp.repeat(draws, shape[dim] // blocks).reshape([-1 if axis == dim else 1 for axis in range(len(shape))])
    return level


def gaussian(own_key, extent, width, bound, split=(), held_as=jnp.bfloat16):
    gain = shard_levels(own_key, extent, split, -0.22, 0.18) if split else 1.0
    array = jax.random.normal(own_key, extent, jnp.float32) * width * gain
    return jnp.minimum(jnp.maximum(array, -bound), bound).astype(held_as)


def setup_inputs(seed: int = 0) -> dict:
    splits = jax.random.split(jax.random.key(seed), 6)
    grad_parts = gaussian(splits[0], (N_REP, D, D), 1.0, 6.0, ((0, 2), (1, 16), (2, 16)))
    basis_left = gaussian(splits[1], (D, D), D ** -0.5, 0.09375, ((0, 32), (1, 16)))
    basis_right = gaussian(splits[2], (D, D), D ** -0.5, 0.09375, ((0, 32), (1, 16)))
    first_moment = gaussian(splits[3], (D, D), 1.0, 6.0, ((0, 32), (1, 16)), jnp.float32)
    second_moment = jnp.clip(jnp.exp(math.log(4.0) - 2.0794415 * jax.random.uniform(splits[4], (D, D), jnp.float32) ** shard_levels(splits[4], (D, D), ((0, 32), (1, 16)), -0.2, 0.2)), 0.5, 4.0)
    return dict(grad_parts=grad_parts, basis_left=basis_left, basis_right=basis_right, first_moment=first_moment, second_moment=second_moment)


BETA_ONE = 0.9
BETA_TWO = 0.95
EPSILON = 1e-08

def reference(grad_parts, basis_left, basis_right, first_moment, second_moment):
    grad_sum = lax.optimization_barrier(jnp.sum(grad_parts.astype(jnp.float32), axis=0)).astype(jnp.bfloat16)
    rotated = jnp.dot(basis_left.T, grad_sum, preferred_element_type=jnp.float32).astype(jnp.bfloat16)
    projected = jnp.dot(rotated, basis_right, preferred_element_type=jnp.float32)
    new_first = BETA_ONE * first_moment + (1.0 - BETA_ONE) * projected
    new_second = BETA_TWO * second_moment + (1.0 - BETA_TWO) * projected * projected
    normed = (new_first / (jnp.sqrt(new_second) + EPSILON)).astype(jnp.bfloat16)
    back_left = jnp.dot(basis_left, normed, preferred_element_type=jnp.float32).astype(jnp.bfloat16)
    update = jnp.dot(back_left, basis_right.T, preferred_element_type=jnp.float32)
    return (update, new_first, new_second)
```

```python
import jax
import jax.numpy as jnp
from jax import lax
from jax.experimental import pallas as pl
from jax.experimental.pallas import tpu as pltpu
from jax.sharding import Mesh, PartitionSpec as P

BETA_ONE = 0.9
BETA_TWO = 0.95
EPSILON = 1e-08

BITS = ("xh", "z2", "z1", "z0", "y2", "y1", "y0", "core", "rep")
ROW = ("xh", "z2", "z1", "z0")
COL = ("y2", "y1", "y0", "core")
F32 = jnp.float32
BF16 = jnp.bfloat16


def move(block, swaps, flips=()):
    pairs = []
    for source in range(2 ** len(BITS)):
        bits = {name: (source >> (len(BITS) - 1 - n)) & 1 for n, name in enumerate(BITS)}
        for one, other in swaps:
            bits[one], bits[other] = bits[other], bits[one]
        for name in flips:
            bits[name] = 1 - bits[name]
        target = 0
        for name in BITS:
            target = target * 2 + bits[name]
        pairs.append((source, target))
    return lax.ppermute(block, BITS, pairs)


def call(kernel, out_shape, *operands, blocks=None):
    blocks = blocks or [None] * len(operands)
    specs = []
    for operand, block in zip(operands, blocks):
        shape, index = block or (operand.shape, (0,) * operand.ndim)
        specs.append(pl.BlockSpec(shape, lambda i, index=index: index))
    return pl.pallas_call(
        kernel,
        grid=(1,),
        out_shape=jax.ShapeDtypeStruct(out_shape, BF16),
        in_specs=specs,
        out_specs=pl.BlockSpec(out_shape, lambda i: (0,) * len(out_shape)),
        compiler_params=pltpu.CompilerParams(vmem_limit_bytes=32 * 2**20),
    )(*operands)


def first_kernel(left_ref, grad_ref, out_ref):
    for block in range(2):
        total = None
        for k in range(8):
            part = lax.dot_general(
                left_ref[k // 4, block, k % 4, 0], grad_ref[k], (((0,), (0,)), ((), ())),
                preferred_element_type=F32,
            )
            total = part if total is None else total + part
        out_ref[block] = total.astype(BF16)


def second_kernel(rotated_ref, right_ref, out_ref):
    for column in range(2):
        total = None
        for k in range(8):
            part = jnp.dot(
                rotated_ref[k], right_ref[k, column], preferred_element_type=F32
            )
            total = part if total is None else total + part
        out_ref[column] = total.astype(BF16)


def third_kernel(left_ref, normed_ref, out_ref):
    for block in range(4):
        total = None
        for k in range(4):
            part = jnp.dot(
                left_ref[k // 2, block, k % 2, 0], normed_ref[k], preferred_element_type=F32
            )
            total = part if total is None else total + part
        out_ref[block] = total.astype(BF16)


def fourth_kernel(back_ref, right_ref, out_ref):
    for column in range(2):
        total = None
        for k in range(8):
            part = lax.dot_general(
                back_ref[k], right_ref[k, column], (((1,), (1,)), ((), ())),
                preferred_element_type=F32,
            )
            total = part if total is None else total + part
        out_ref[column] = total.astype(BF16)


def exchange(parts, axes):
    return jnp.sum(lax.all_to_all(parts, axes, 0, 0).astype(F32), axis=0)


def spread(block, axes):
    copies = 2 ** len(axes)
    return lax.all_to_all(jnp.broadcast_to(block[None], (copies,) + block.shape), axes, 0, 0)


def on_device(grad_parts, basis_left, basis_right, first_moment, second_moment):
    half = basis_left.shape[0]
    width = basis_left.shape[1]
    grad = grad_parts[0]
    rep = lax.axis_index("rep")

    left = jnp.concatenate(
        [
            move(basis_left, [("z2", "y1")]),
            move(basis_left, [("xh", "y2"), ("z0", "core")]),
        ]
    )
    left = lax.all_gather(left, ("y2", "y1", "y0", "core"))

    own = lax.dynamic_slice_in_dim(grad, rep * half, half, 0)
    other = lax.dynamic_slice_in_dim(grad, (1 - rep) * half, half, 0)
    grad_half = (own.astype(F32) + move(other, [], ["rep"]).astype(F32)).astype(BF16)
    grad_panel = spread(grad_half, ("xh", "z1", "z0"))

    right = jnp.concatenate(
        [
            move(basis_right, [("xh", "y2")]),
            move(basis_right, [("z2", "y1"), ("z1", "y0"), ("z0", "core")]),
        ]
    )
    right = lax.all_gather(right, ("xh", "rep"))
    right_second = lax.all_gather(right[:, :half], ("z2", "z1", "z0"))
    right_second = right_second.reshape(8, 2, width, width)

    parts = call(
        first_kernel, (2, width, width),
        left.reshape(2, 2, 4, 2, half, width), grad_panel,
        blocks=[((2, 2, 4, 1, half, width), (0, 0, 0, 0, 0, 0)), None],
    )
    rotated = exchange(parts.reshape(4, half, width), ("z2", "rep")).astype(BF16)
    rotated, right = lax.optimization_barrier((rotated, right))
    right_fourth = lax.all_gather(right[:, half:], ("z2", "z1", "z0"))
    right_fourth = right_fourth.reshape(8, 2, width, width)
    rotated_panel = lax.all_gather(rotated, ("y1", "y0", "core"))

    parts = call(second_kernel, (2, half, width), rotated_panel, right_second)
    projected = exchange(parts, ("y2",))

    new_first = BETA_ONE * first_moment + (1.0 - BETA_ONE) * projected
    new_second = BETA_TWO * second_moment + (1.0 - BETA_TWO) * projected * projected
    normed = (new_first / (jnp.sqrt(new_second) + EPSILON)).astype(BF16)
    normed_panel = spread(normed, ("xh", "z0", "rep")).reshape(4, width, width)

    parts = call(
        third_kernel, (4, half, width),
        left.reshape(2, 4, 2, 2, half, width), normed_panel,
        blocks=[((2, 4, 2, 1, half, width), (0, 0, 0, 1, 0, 0)), None],
    )
    back_left = exchange(parts, ("z2", "z1")).astype(BF16)
    back_panel = lax.all_gather(back_left, ("y1", "y0", "core"))

    parts = call(fourth_kernel, (2, half, width), back_panel, right_fourth)
    update = exchange(parts, ("y2",))
    return (update, new_first, new_second)


def solution(mesh):
    bits = Mesh(mesh.devices.reshape((2,) * len(BITS)), BITS)
    block = P(ROW + ("rep",), COL)
    in_specs = (P("rep", ROW, COL), P(COL + ("rep",), ROW), block, block, block)
    return jax.shard_map(
        on_device, mesh=bits, in_specs=in_specs, out_specs=(block,) * 3, check_vma=False
    )
```

```python
import jax
import jax.numpy as jnp
from jax import lax
from jax.experimental import pallas as pl
from jax.experimental.pallas import tpu as pltpu
from jax.sharding import Mesh, PartitionSpec as P

BETA_ONE = 0.9
BETA_TWO = 0.95
EPSILON = 1e-08

BITS = ("xh", "z2", "z1", "z0", "y2", "y1", "y0", "core", "rep")
ROW = ("xh", "z2", "z1", "z0")
COL = ("y2", "y1", "y0", "core")
F32 = jnp.float32
BF16 = jnp.bfloat16


def move(block, swaps, flips=()):
    pairs = []
    for source in range(2 ** len(BITS)):
        bits = {name: (source >> (len(BITS) - 1 - n)) & 1 for n, name in enumerate(BITS)}
        for one, other in swaps:
            bits[one], bits[other] = bits[other], bits[one]
        for name in flips:
            bits[name] = 1 - bits[name]
        target = 0
        for name in BITS:
            target = target * 2 + bits[name]
        pairs.append((source, target))
    return lax.ppermute(block, BITS, pairs)


def call(kernel, out_shape, *operands):
    return pl.pallas_call(
        kernel,
        out_shape=jax.ShapeDtypeStruct(out_shape, BF16),
        in_specs=[pl.BlockSpec(memory_space=pltpu.VMEM)] * len(operands),
        out_specs=pl.BlockSpec(memory_space=pltpu.VMEM),
        compiler_params=pltpu.CompilerParams(vmem_limit_bytes=32 * 2**20),
    )(*operands)


def first_kernel(left_ref, grad_ref, out_ref):
    for block in range(4):
        total = None
        for k in range(4):
            part = lax.dot_general(
                left_ref[block // 2, k, block % 2], grad_ref[k], (((0,), (0,)), ((), ())),
                preferred_element_type=F32,
            )
            total = part if total is None else total + part
        out_ref[block] = total.astype(BF16)


def second_kernel(rotated_ref, right_ref, out_ref):
    for block in range(4):
        total = None
        for k in range(4):
            part = jnp.dot(
                rotated_ref[k], right_ref[block % 2, k, block // 2],
                preferred_element_type=F32,
            )
            total = part if total is None else total + part
        out_ref[block] = total.astype(BF16)


def third_kernel(left_ref, normed_ref, out_ref):
    for block in range(4):
        total = None
        for k in range(4):
            part = jnp.dot(
                left_ref[k // 2, block, k % 2], normed_ref[k], preferred_element_type=F32
            )
            total = part if total is None else total + part
        out_ref[block] = total.astype(BF16)


def fourth_kernel(back_ref, right_ref, out_ref):
    for block in range(4):
        total = None
        for k in range(4):
            part = lax.dot_general(
                back_ref[k], right_ref[k % 2, block, k // 2], (((1,), (1,)), ((), ())),
                preferred_element_type=F32,
            )
            total = part if total is None else total + part
        out_ref[block] = total.astype(BF16)


def exchange(parts, axes):
    return jnp.sum(lax.all_to_all(parts, axes, 0, 0).astype(F32), axis=0)


def spread(block, axes):
    copies = 2 ** len(axes)
    return lax.all_to_all(jnp.broadcast_to(block[None], (copies,) + block.shape), axes, 0, 0)


def on_device(grad_parts, basis_left, basis_right, first_moment, second_moment):
    half = basis_left.shape[0]
    width = basis_left.shape[1]
    grad = grad_parts[0]
    rep = lax.axis_index("rep")

    left = move(basis_left, [("xh", "y2"), ("z0", "core")])
    left = lax.all_gather(left, ("y2", "y1", "y0", "core"))
    left = left.reshape(2, 4, 2, half, width)

    right = move(basis_right, [("xh", "y2"), ("z2", "y1")])
    right = lax.all_gather(right, ("xh", "rep"))
    right = lax.all_gather(right, ("z2", "z1", "z0"))
    right = right.reshape(2, 4, 2, width, width)

    own = lax.dynamic_slice_in_dim(grad, rep * half, half, 0)
    other = lax.dynamic_slice_in_dim(grad, (1 - rep) * half, half, 0)
    grad_half = (own.astype(F32) + move(other, [], ["rep"]).astype(F32)).astype(BF16)

    grad_panel = spread(grad_half, ("z2", "z1"))
    parts = call(first_kernel, (4, width, width), left, grad_panel)
    parts = parts.reshape(8, half, width)
    rotated = exchange(parts, ("xh", "z0", "rep")).astype(BF16)

    rotated_panel = lax.all_gather(rotated, ("y0", "core"))
    parts = call(second_kernel, (4, half, width), rotated_panel, right)
    projected = exchange(parts, ("y2", "y1"))

    new_first = BETA_ONE * first_moment + (1.0 - BETA_ONE) * projected
    new_second = BETA_TWO * second_moment + (1.0 - BETA_TWO) * projected * projected
    normed = (new_first / (jnp.sqrt(new_second) + EPSILON)).astype(BF16)

    normed_panel = spread(normed, ("xh", "z0", "rep")).reshape(4, width, width)
    parts = call(third_kernel, (4, half, width), left, normed_panel)
    back_left = exchange(parts, ("z2", "z1")).astype(BF16)

    back_panel = lax.all_gather(back_left, ("y2", "y1"))
    parts = call(fourth_kernel, (4, half, width), back_panel, right)
    update = exchange(parts, ("y0", "core"))
    return (update, new_first, new_second)


def solution(mesh):
    bits = Mesh(mesh.devices.reshape((2,) * len(BITS)), BITS)
    block = P(ROW + ("rep",), COL)
    in_specs = (P("rep", ROW, COL), P(COL + ("rep",), ROW), block, block, block)
    return jax.shard_map(
        on_device, mesh=bits, in_specs=in_specs, out_specs=(block,) * 3, check_vma=False
    )
```

```python
import jax
import jax.numpy as jnp
from jax import lax
from jax.experimental import pallas as pl
from jax.experimental.pallas import tpu as pltpu
from jax.sharding import Mesh, PartitionSpec as P

BETA_ONE = 0.9
BETA_TWO = 0.95
EPSILON = 1e-08

BITS = ("xh", "z2", "z1", "z0", "y2", "y1", "y0", "core", "rep")
ROW = ("xh", "z2", "z1", "z0")
COL = ("y2", "y1", "y0", "core")
F32 = jnp.float32
BF16 = jnp.bfloat16


def move(block, swaps, flips=()):
    pairs = []
    for source in range(2 ** len(BITS)):
        bits = {name: (source >> (len(BITS) - 1 - n)) & 1 for n, name in enumerate(BITS)}
        for one, other in swaps:
            bits[one], bits[other] = bits[other], bits[one]
        for name in flips:
            bits[name] = 1 - bits[name]
        target = 0
        for name in BITS:
            target = target * 2 + bits[name]
        pairs.append((source, target))
    return lax.ppermute(block, BITS, pairs)


def call(kernel, out_shape, *operands):
    return pl.pallas_call(
        kernel,
        out_shape=jax.ShapeDtypeStruct(out_shape, BF16),
        in_specs=[pl.BlockSpec(memory_space=pltpu.VMEM)] * len(operands),
        out_specs=pl.BlockSpec(memory_space=pltpu.VMEM),
        compiler_params=pltpu.CompilerParams(vmem_limit_bytes=32 * 2**20),
    )(*operands)


def first_kernel(left_ref, grad_ref, out_ref):
    for block in range(4):
        total = None
        for k in range(4):
            part = lax.dot_general(
                left_ref[block // 2, k, block % 2], grad_ref[k], (((0,), (0,)), ((), ())),
                preferred_element_type=F32,
            )
            total = part if total is None else total + part
        out_ref[block] = total.astype(BF16)


def second_kernel(rotated_ref, right_ref, out_ref):
    for block in range(4):
        total = None
        for k in range(4):
            part = jnp.dot(
                rotated_ref[k], right_ref[k % 2, block, k // 2],
                preferred_element_type=F32,
            )
            total = part if total is None else total + part
        out_ref[block] = total.astype(BF16)


def third_kernel(left_ref, normed_ref, out_ref):
    for block in range(4):
        total = None
        for k in range(4):
            part = jnp.dot(
                left_ref[k // 2, block, k % 2], normed_ref[k], preferred_element_type=F32
            )
            total = part if total is None else total + part
        out_ref[block] = total.astype(BF16)


def fourth_kernel(back_ref, right_ref, out_ref):
    for block in range(4):
        total = None
        for k in range(4):
            part = lax.dot_general(
                back_ref[k], right_ref[block % 2, k, block // 2], (((1,), (1,)), ((), ())),
                preferred_element_type=F32,
            )
            total = part if total is None else total + part
        out_ref[block] = total.astype(BF16)


def exchange(parts, axes):
    return jnp.sum(lax.all_to_all(parts, axes, 0, 0).astype(F32), axis=0)


def spread(block, axes):
    copies = 2 ** len(axes)
    return lax.all_to_all(jnp.broadcast_to(block[None], (copies,) + block.shape), axes, 0, 0)


def on_device(grad_parts, basis_left, basis_right, first_moment, second_moment):
    half = basis_left.shape[0]
    width = basis_left.shape[1]
    grad = grad_parts[0]
    rep = lax.axis_index("rep")

    left = move(basis_left, [("xh", "y2"), ("z0", "core")])
    left = lax.all_gather(left, ("y2", "y1", "y0", "core"))
    left = left.reshape(2, 4, 2, half, width)

    own = lax.dynamic_slice_in_dim(grad, rep * half, half, 0)
    other = lax.dynamic_slice_in_dim(grad, (1 - rep) * half, half, 0)
    other = move(other, [], ["rep"])
    right = move(basis_right, [("z1", "y0"), ("z0", "core")])
    other, right = lax.optimization_barrier((other, right))
    right = lax.all_gather(right, ("xh", "rep"))
    right = lax.all_gather(right, ("z2", "z1", "z0"))
    right = right.reshape(2, 4, 2, width, width)
    grad_half = (own.astype(F32) + other.astype(F32)).astype(BF16)

    grad_panel = spread(grad_half, ("z2", "z1"))
    parts = call(first_kernel, (4, width, width), left, grad_panel)
    parts = parts.reshape(8, half, width)
    rotated = exchange(parts, ("xh", "z0", "rep")).astype(BF16)

    rotated_panel = lax.all_gather(rotated, ("y2", "y1"))
    parts = call(second_kernel, (4, half, width), rotated_panel, right)
    projected = exchange(parts, ("y0", "core"))

    new_first = BETA_ONE * first_moment + (1.0 - BETA_ONE) * projected
    new_second = BETA_TWO * second_moment + (1.0 - BETA_TWO) * projected * projected
    normed = (new_first / (jnp.sqrt(new_second) + EPSILON)).astype(BF16)

    normed_panel = spread(normed, ("xh", "z0", "rep")).reshape(4, width, width)
    parts = call(third_kernel, (4, half, width), left, normed_panel)
    back_left = exchange(parts, ("z2", "z1")).astype(BF16)

    back_panel = lax.all_gather(back_left, ("y0", "core"))
    parts = call(fourth_kernel, (4, half, width), back_panel, right)
    update = exchange(parts, ("y2", "y1"))
    return (update, new_first, new_second)


def solution(mesh):
    bits = Mesh(mesh.devices.reshape((2,) * len(BITS)), BITS)
    block = P(ROW + ("rep",), COL)
    in_specs = (P("rep", ROW, COL), P(COL + ("rep",), ROW), block, block, block)
    return jax.shard_map(
        on_device, mesh=bits, in_specs=in_specs, out_specs=(block,) * 3, check_vma=False
    )
```

```python
import jax
import jax.numpy as jnp
from jax import lax
from jax.experimental import pallas as pl
from jax.experimental.pallas import tpu as pltpu
from jax.sharding import Mesh, PartitionSpec as P

BETA_ONE = 0.9
BETA_TWO = 0.95
EPSILON = 1e-08

BITS = ("xh", "z2", "z1", "z0", "y2", "y1", "y0", "core", "rep")
ROW = ("xh", "z2", "z1", "z0")
COL = ("y2", "y1", "y0", "core")
F32 = jnp.float32
BF16 = jnp.bfloat16


def move(block, swaps, flips=()):
    pairs = []
    for source in range(2 ** len(BITS)):
        bits = {name: (source >> (len(BITS) - 1 - n)) & 1 for n, name in enumerate(BITS)}
        for one, other in swaps:
            bits[one], bits[other] = bits[other], bits[one]
        for name in flips:
            bits[name] = 1 - bits[name]
        target = 0
        for name in BITS:
            target = target * 2 + bits[name]
        pairs.append((source, target))
    return lax.ppermute(block, BITS, pairs)


def call(kernel, out_shape, *operands):
    return pl.pallas_call(
        kernel,
        out_shape=jax.ShapeDtypeStruct(out_shape, BF16),
        in_specs=[pl.BlockSpec(memory_space=pltpu.VMEM)] * len(operands),
        out_specs=pl.BlockSpec(memory_space=pltpu.VMEM),
        compiler_params=pltpu.CompilerParams(vmem_limit_bytes=32 * 2**20),
    )(*operands)


def first_kernel(left_ref, grad_ref, out_ref):
    for block in range(4):
        total = None
        for k in range(4):
            part = lax.dot_general(
                left_ref[block // 2, k, block % 2], grad_ref[k], (((0,), (0,)), ((), ())),
                preferred_element_type=F32,
            )
            total = part if total is None else total + part
        out_ref[block] = total.astype(BF16)


def second_kernel(rotated_ref, right_ref, out_ref):
    for block in range(2):
        total = None
        for k in range(8):
            part = jnp.dot(
                rotated_ref[k], right_ref[k % 4, block, k // 4],
                preferred_element_type=F32,
            )
            total = part if total is None else total + part
        out_ref[block] = total.astype(BF16)


def third_kernel(left_ref, normed_ref, out_ref):
    rows, width = left_ref.shape[3:]
    total = None
    for k in range(4):
        part = jnp.dot(
            left_ref[k // 2, :, k % 2].reshape(4 * rows, width), normed_ref[k],
            preferred_element_type=F32,
        )
        total = part if total is None else total + part
    out_ref[...] = total.astype(BF16).reshape(4, rows, width)


def fourth_kernel(back_ref, right_ref, out_ref):
    for block in range(8):
        total = None
        for k in range(2):
            part = lax.dot_general(
                back_ref[k], right_ref[block % 4, k, block // 4], (((1,), (1,)), ((), ())),
                preferred_element_type=F32,
            )
            total = part if total is None else total + part
        out_ref[block] = total.astype(BF16)


def exchange(parts, axes):
    return jnp.sum(lax.all_to_all(parts, axes, 0, 0).astype(F32), axis=0)


def spread(block, axes):
    copies = 2 ** len(axes)
    return lax.all_to_all(jnp.broadcast_to(block[None], (copies,) + block.shape), axes, 0, 0)


def on_device(grad_parts, basis_left, basis_right, first_moment, second_moment):
    half = basis_left.shape[0]
    width = basis_left.shape[1]
    grad = grad_parts[0]
    rep = lax.axis_index("rep")

    left = move(basis_left, [("xh", "y2"), ("z0", "core")])
    left = lax.all_gather(left, ("y2", "y1", "y0", "core"))
    left = left.reshape(2, 4, 2, half, width)

    own = lax.dynamic_slice_in_dim(grad, rep * half, half, 0)
    other = lax.dynamic_slice_in_dim(grad, (1 - rep) * half, half, 0)
    other = move(other, [], ["rep"])
    right = move(basis_right, [("z0", "core")])
    other, right = lax.optimization_barrier((other, right))
    right = lax.all_gather(right, ("xh", "rep"))
    right = lax.all_gather(right, ("z2", "z1", "z0"))
    right = right.reshape(4, 2, 2, width, width)
    grad_half = (own.astype(F32) + other.astype(F32)).astype(BF16)

    grad_panel = spread(grad_half, ("z2", "z1"))
    parts = call(first_kernel, (4, width, width), left, grad_panel)
    parts = parts.reshape(8, half, width)
    rotated = exchange(parts, ("xh", "z0", "rep")).astype(BF16)

    rotated_panel = lax.all_gather(rotated, ("y2", "y1", "y0"))
    parts = call(second_kernel, (2, half, width), rotated_panel, right)
    projected = exchange(parts, ("core",))

    new_first = BETA_ONE * first_moment + (1.0 - BETA_ONE) * projected
    new_second = BETA_TWO * second_moment + (1.0 - BETA_TWO) * projected * projected
    normed = (new_first / (jnp.sqrt(new_second) + EPSILON)).astype(BF16)

    normed_panel = spread(normed, ("xh", "z0", "rep")).reshape(4, width, width)
    parts = call(third_kernel, (4, half, width), left, normed_panel)
    back_left = exchange(parts, ("z2", "z1")).astype(BF16)

    back_panel = lax.all_gather(back_left, ("core",))
    parts = call(fourth_kernel, (8, half, width), back_panel, right)
    update = exchange(parts, ("y2", "y1", "y0"))
    return (update, new_first, new_second)


def solution(mesh):
    bits = Mesh(mesh.devices.reshape((2,) * len(BITS)), BITS)
    block = P(ROW + ("rep",), COL)
    in_specs = (P("rep", ROW, COL), P(COL + ("rep",), ROW), block, block, block)
    return jax.shard_map(
        on_device, mesh=bits, in_specs=in_specs, out_specs=(block,) * 3, check_vma=False
    )
```

```python
import jax
import jax.numpy as jnp
from jax import lax
from jax.experimental import pallas as pl
from jax.experimental.pallas import tpu as pltpu
from jax.sharding import Mesh, PartitionSpec as P

BETA_ONE = 0.9
BETA_TWO = 0.95
EPSILON = 1e-08

BITS = ("xh", "z2", "z1", "z0", "y2", "y1", "y0", "core", "rep")
ROW = ("xh", "z2", "z1", "z0")
COL = ("y2", "y1", "y0", "core")
F32 = jnp.float32
BF16 = jnp.bfloat16


def move(block, swaps, flips=()):
    pairs = []
    for source in range(2 ** len(BITS)):
        bits = {name: (source >> (len(BITS) - 1 - n)) & 1 for n, name in enumerate(BITS)}
        for one, other in swaps:
            bits[one], bits[other] = bits[other], bits[one]
        for name in flips:
            bits[name] = 1 - bits[name]
        target = 0
        for name in BITS:
            target = target * 2 + bits[name]
        pairs.append((source, target))
    return lax.ppermute(block, BITS, pairs)


def call(kernel, out_shape, *operands):
    return pl.pallas_call(
        kernel,
        out_shape=jax.ShapeDtypeStruct(out_shape, BF16),
        in_specs=[pl.BlockSpec(memory_space=pltpu.VMEM)] * len(operands),
        out_specs=pl.BlockSpec(memory_space=pltpu.VMEM),
        compiler_params=pltpu.CompilerParams(vmem_limit_bytes=32 * 2**20),
    )(*operands)


def first_kernel(left_ref, grad_ref, out_ref):
    for block in range(4):
        total = None
        for k in range(4):
            part = lax.dot_general(
                left_ref[block // 2, k, block % 2], grad_ref[k], (((0,), (0,)), ((), ())),
                preferred_element_type=F32,
            )
            total = part if total is None else total + part
        out_ref[block] = total.astype(BF16)


def second_kernel(rotated_ref, right_ref, out_ref, held_ref, sems):
    copies = [
        pltpu.make_async_copy(right_ref.at[:, block], held_ref.at[block], sems.at[block])
        for block in range(2)
    ]
    for copy in copies:
        copy.start()
    for block in range(2):
        copies[block].wait()
        total = None
        for k in range(8):
            part = jnp.dot(
                rotated_ref[k], held_ref[block, k % 4, k // 4], preferred_element_type=F32
            )
            total = part if total is None else total + part
        out_ref[block] = total.astype(BF16)


def second(rotated, right):
    _, rows, width = rotated.shape
    return pl.pallas_call(
        second_kernel,
        out_shape=jax.ShapeDtypeStruct((2, rows, width), BF16),
        in_specs=[
            pl.BlockSpec(memory_space=pltpu.VMEM),
            pl.BlockSpec(memory_space=pltpu.HBM),
        ],
        out_specs=pl.BlockSpec(memory_space=pltpu.VMEM),
        scratch_shapes=[
            pltpu.VMEM((2, 4, 2, width, width), BF16),
            pltpu.SemaphoreType.DMA((2,)),
        ],
        compiler_params=pltpu.CompilerParams(vmem_limit_bytes=32 * 2**20),
    )(rotated, right)


def third_kernel(left_ref, normed_ref, out_ref):
    rows, width = left_ref.shape[3:]
    total = None
    for k in range(4):
        part = jnp.dot(
            left_ref[k // 2, :, k % 2].reshape(4 * rows, width), normed_ref[k],
            preferred_element_type=F32,
        )
        total = part if total is None else total + part
    out_ref[...] = total.astype(BF16).reshape(4, rows, width)


def fourth_kernel(back_ref, right_ref, out_ref):
    for block in range(8):
        total = None
        for k in range(2):
            part = lax.dot_general(
                back_ref[k], right_ref[block % 4, k, block // 4], (((1,), (1,)), ((), ())),
                preferred_element_type=F32,
            )
            total = part if total is None else total + part
        out_ref[block] = total.astype(BF16)


def exchange(parts, axes):
    return jnp.sum(lax.all_to_all(parts, axes, 0, 0).astype(F32), axis=0)


def spread(block, axes):
    copies = 2 ** len(axes)
    return lax.all_to_all(jnp.broadcast_to(block[None], (copies,) + block.shape), axes, 0, 0)


def on_device(grad_parts, basis_left, basis_right, first_moment, second_moment):
    half = basis_left.shape[0]
    width = basis_left.shape[1]
    grad = grad_parts[0]
    rep = lax.axis_index("rep")

    left = move(basis_left, [("xh", "y2"), ("z0", "core")])
    left = lax.all_gather(left, ("y2", "y1", "y0", "core"))
    left = left.reshape(2, 4, 2, half, width)

    own = lax.dynamic_slice_in_dim(grad, rep * half, half, 0)
    other = lax.dynamic_slice_in_dim(grad, (1 - rep) * half, half, 0)
    other = move(other, [], ["rep"])
    right = move(basis_right, [("z0", "core")])
    other, right = lax.optimization_barrier((other, right))
    right = lax.all_gather(right, ("xh", "rep"))
    right = lax.all_gather(right, ("z2", "z1", "z0"))
    right = right.reshape(4, 2, 2, width, width)
    grad_half = (own.astype(F32) + other.astype(F32)).astype(BF16)

    grad_panel = spread(grad_half, ("z2", "z1"))
    parts = call(first_kernel, (4, width, width), left, grad_panel)
    parts = parts.reshape(8, half, width)
    rotated = exchange(parts, ("xh", "z0", "rep")).astype(BF16)

    rotated_panel = lax.all_gather(rotated, ("y2", "y1", "y0"))
    parts = second(rotated_panel, right)
    projected = exchange(parts, ("core",))
    right, projected = lax.optimization_barrier((right, projected))

    new_first = BETA_ONE * first_moment + (1.0 - BETA_ONE) * projected
    new_second = BETA_TWO * second_moment + (1.0 - BETA_TWO) * projected * projected
    normed = (new_first / (jnp.sqrt(new_second) + EPSILON)).astype(BF16)

    normed_panel = spread(normed, ("xh", "z0", "rep")).reshape(4, width, width)
    parts = call(third_kernel, (4, half, width), left, normed_panel)
    back_left = exchange(parts, ("z2", "z1")).astype(BF16)

    back_panel = lax.all_gather(back_left, ("core",))
    parts = call(fourth_kernel, (8, half, width), back_panel, right)
    update = exchange(parts, ("y2", "y1", "y0"))
    return (update, new_first, new_second)


def solution(mesh):
    bits = Mesh(mesh.devices.reshape((2,) * len(BITS)), BITS)
    block = P(ROW + ("rep",), COL)
    in_specs = (P("rep", ROW, COL), P(COL + ("rep",), ROW), block, block, block)
    return jax.shard_map(
        on_device, mesh=bits, in_specs=in_specs, out_specs=(block,) * 3, check_vma=False
    )
```
